32 devices in a mesh: gx: 4 (over y, x), gy: 8 (over z, core).
Axes of the slice: x: 2, y: 2, z: 4, core: 2. Of those that a mesh axis runs over, the one named last changes fastest.
Arguments:
- forcing: float32 [4, 2, 256, 1024], P(None, None, 'gx', 'gy'), may hold values from -18 to 18
- observed: float32 [4, 2, 256, 1024], P(None, None, 'gx', 'gy'), may hold values from -6 to 6
- viscosity: float32 [256, 1024], P('gx', 'gy'), may hold values from 0.05 to 0.5
- friction: float32 [256, 1024], P('gx', 'gy'), may hold values from 0.2 to 2
- ice_mask: int32 [256, 1024], P('gx', 'gy'), may hold values from 0 to 2
- dirichlet: int32 [256, 1024], P('gx', 'gy'), may hold values 0 or 1
Outputs:
- velocity: float32 [4, 2, 256, 1024], P(None, None, 'gx', 'gy')
- gradient: float32 [256, 1024], P('gx', 'gy')
The draws below stay inside these ranges and needn't reach their ends.
All inputs are finite; a program needn't handle non-finite values. No bound on the sum of `dirichlet` on one device may be relied on, other than what follows from the above.
Results may differ from the reference program's by a relative error of at most 0.00002.
Values sent between devices are 32-bit elements; how exact they have to be, the bound alone decides.
A program may use at most 64 MiB of HBM per device.

```python
import math
import jax
import jax.numpy as jnp

EPOCHS = 4
SWEEPS = 3
NX = 256
NY = 1024


def place_ends(entries, key, least, top_value):
    place = [jax.random.randint(jax.random.fold_in(key, axis), (), 0, length) for axis, length in enumerate(entries.shape)]
    widest = entries.shape.index(max(entries.shape))
    neighbour = place[:widest] + [(place[widest] + 1) % entries.shape[widest]] + place[widest + 1:]
    return entries.at[tuple(place)].set(least).at[tuple(neighbour)].set(top_value)


def levels(key, shape, pieces, smallest, top_value):
    factor_of = 1.0
    for axis_at, blocks in pieces:
        steps = jax.random.uniform(jax.random.fold_in(jax.random.fold_in(key, 6), axis_at), (blocks,), jnp.float32, smallest / len(pieces), top_value / len(pieces))
        factor_of = factor_of * jnp.repeat(jnp.exp(steps), shape[axis_at] // blocks).reshape((-1,) + (1,) * (len(shape) - 1 - axis_at))
    return factor_of


def scatter_about(rng, dims, spread, limit, cuts=(), held_as=jnp.bfloat16):
    array = spread * jax.random.normal(rng, dims, jnp.float32)
    if cuts:
        array = array * levels(rng, dims, cuts, -0.22, 0.18)
    return jnp.clip(array, -limit, limit).astype(held_as)


def setup_inputs(seed: int = 0) -> dict:
    seeds = jax.random.split(jax.random.key(seed), 7)
    return {
        "forcing": scatter_about(seeds[0], (EPOCHS, 2, NX, NY), 3.0, 18.0, ((2, 4), (3, 8)), jnp.float32),
        "observed": scatter_about(seeds[1], (EPOCHS, 2, NX, NY), 1.0, 6.0, ((2, 4), (3, 8)), jnp.float32),
        "viscosity": jnp.clip(jnp.exp(math.log(0.5) - 2.3025851 * jax.random.uniform(seeds[2], (NX, NY), jnp.float32) ** levels(seeds[2], (NX, NY), ((0, 4), (1, 8)), -0.2, 0.2)), 0.05, 0.5),
        "friction": jnp.clip(jnp.exp(math.log(2.0) - 2.3025851 * jax.random.uniform(seeds[3], (NX, NY), jnp.float32) ** levels(seeds[3], (NX, NY), ((0, 4), (1, 8)), -0.2, 0.2)), 0.2, 2.0),
        "ice_mask": place_ends(jax.random.randint(seeds[4], (NX, NY), 0, 3), jax.random.fold_in(seeds[4], 1), 0, 2).astype(jnp.int32),
        "dirichlet": place_ends((jax.random.randint(seeds[5], (NX, NY), 0, 16) < 1).astype(jnp.int32), jax.random.fold_in(seeds[5], 1), 0, 1),
    }


UPPER_BOUND = 2.4
LOWER_BOUND = 0.05
FREE_DRAG = 4.0


def face_values(eta_ext):
    centre = eta_ext[1:-1, 1:-1]
    north = eta_ext[2:, 1:-1]
    south = eta_ext[:-2, 1:-1]
    east = eta_ext[1:-1, 2:]
    west = eta_ext[1:-1, :-2]
    return north, south, east, west, 0.5 * (centre + north), 0.5 * (centre + south), 0.5 * (centre + east), 0.5 * (centre + west)


def stencil_apply(field, eta_ext, node_drag):
    north, south, east, west, face_np, face_sm, face_ep, face_wm = face_values(eta_ext)
    along_u = field[:, 0]
    along_v = field[:, 1]

    def normal_part(values, weight_rows, weight_cols):
        middle = values[:, 1:-1, 1:-1]
        rows_part = face_np * (values[:, 2:, 1:-1] - middle) - face_sm * (middle - values[:, :-2, 1:-1])
        cols_part = face_ep * (values[:, 1:-1, 2:] - middle) - face_wm * (middle - values[:, 1:-1, :-2])
        return weight_rows * rows_part + weight_cols * cols_part

    def cross_part(values, weight_rows, weight_cols):
        slope_cols = 0.5 * (values[:, :, 2:] - values[:, :, :-2])
        slope_rows = 0.5 * (values[:, 2:, :] - values[:, :-2, :])
        first = 0.5 * weight_rows * (north * slope_cols[:, 2:, :] - south * slope_cols[:, :-2, :])
        second = 0.5 * weight_cols * (east * slope_rows[:, :, 2:] - west * slope_rows[:, :, :-2])
        return first + second

    image_u = node_drag * along_u[:, 1:-1, 1:-1] - normal_part(along_u, 4.0, 1.0) - cross_part(along_v, 2.0, 1.0)
    image_v = node_drag * along_v[:, 1:-1, 1:-1] - normal_part(along_v, 1.0, 4.0) - cross_part(along_u, 1.0, 2.0)
    return jnp.stack([image_u, image_v], axis=1)


def diagonal_terms(eta_ext, node_drag):
    north, south, east, west, face_np, face_sm, face_ep, face_wm = face_values(eta_ext)
    rows_sum = face_np + face_sm
    cols_sum = face_ep + face_wm
    return jnp.stack([4.0 * rows_sum + cols_sum + node_drag, rows_sum + 4.0 * cols_sum + node_drag], axis=0)


def chebyshev_sweeps(rhs, eta_pad, node_drag, inverse_diag):
    centre_value = 0.5 * (UPPER_BOUND + LOWER_BOUND)
    half_width = 0.5 * (UPPER_BOUND - LOWER_BOUND)
    ratio_value = centre_value / half_width
    weight_now = 1.0 / ratio_value
    residual = rhs
    direction = inverse_diag * residual / centre_value
    iterate = jnp.zeros_like(rhs)
    for sweep_no in range(SWEEPS + 1):
        iterate = iterate + direction
        if sweep_no < SWEEPS:
            padded = jnp.pad(direction, ((0, 0), (0, 0), (1, 1), (1, 1)))
            residual = residual - stencil_apply(padded, eta_pad, node_drag)
            weight_next = 1.0 / (2.0 * ratio_value - weight_now)
            direction = (weight_next * weight_now) * direction + (2.0 * weight_next / half_width) * (inverse_diag * residual)
            weight_now = weight_next
    return iterate


def reference(forcing, observed, viscosity, friction, ice_mask, dirichlet):
    release = (1 - dirichlet).astype(jnp.float32)
    element_drag = jnp.where(ice_mask == 2, friction, jnp.where(ice_mask == 0, FREE_DRAG, 0.0)).astype(jnp.float32)
    drag_pad = jnp.pad(element_drag, ((1, 0), (1, 0)))
    node_drag = 0.25 * (drag_pad[:-1, :-1] + drag_pad[1:, :-1] + drag_pad[:-1, 1:] + drag_pad[1:, 1:])
    eta_pad = jnp.pad(viscosity, 1)
    inverse_diag = release / (diagonal_terms(eta_pad, node_drag) + 1.0 - release)
    velocity = chebyshev_sweeps(release * forcing, eta_pad, node_drag, inverse_diag)
    misfit = release * (velocity - observed)
    adjoint = chebyshev_sweeps(misfit, eta_pad, node_drag, inverse_diag)
    product = jnp.sum(adjoint * velocity, axis=(0, 1))
    prod_pad = jnp.pad(product, ((0, 1), (0, 1)))
    rows_sum = prod_pad[:-1] + prod_pad[1:]
    total = rows_sum[:, :-1] + rows_sum[:, 1:]
    grounded = (ice_mask == 2).astype(jnp.float32)
    gradient = -0.25 * grounded * total
    return velocity, gradient
```

```python
import jax
import jax.numpy as jnp
from jax import lax
from jax.experimental import pallas as pl
from jax.experimental.pallas import tpu as pltpu
from jax.sharding import PartitionSpec as P

SWEEPS = 3
UPPER_BOUND = 2.4
LOWER_BOUND = 0.05
FREE_DRAG = 4.0
HALO = 8
LANES = 128
EP = 4
NCOEF = 20
MESH = pl.DeviceIdType.MESH
DIRS = ((-1, 0), (1, 0), (0, -1), (0, 1), (-1, -1), (-1, 1), (1, -1), (1, 1))


def chebyshev_weights():
    centre = 0.5 * (UPPER_BOUND + LOWER_BOUND)
    half = 0.5 * (UPPER_BOUND - LOWER_BOUND)
    ratio = centre / half
    now = 1.0 / ratio
    pairs = []
    for _ in range(SWEEPS):
        following = 1.0 / (2.0 * ratio - now)
        pairs.append((following * now, 2.0 * following / half))
        now = following
    return 1.0 / centre, pairs


def kernel(rows, forcing, observed, visc, fric, mask, dirich, vel_out, grad_out,
           F, O, K, FM, IM, DM, PK, PS, E, FRV, KF, D, R, X, B2, VO, PD, PT, GO,
           lsem, osem, ssem, rsem):
    gx, gy = lax.axis_index("gx"), lax.axis_index("gy")
    nx, ny = lax.axis_size("gx"), lax.axis_size("gy")
    ext = rows + 2 * HALO
    tiles = ext // 8
    own_tiles = rows // 8
    end = rows + HALO

    def has(dx, dy):
        cond = None
        for idx, size, step in ((gx, nx, dx), (gy, ny, dy)):
            if step:
                here = idx > 0 if step < 0 else idx < size - 1
                cond = here if cond is None else jnp.logical_and(cond, here)
        return cond

    def lacks(dx, dy):
        return jnp.logical_not(has(dx, dy))

    loads = [
        pltpu.make_async_copy(visc, K.at[0, pl.ds(HALO, rows)], lsem.at[0]),
        pltpu.make_async_copy(fric, FM, lsem.at[1]),
        pltpu.make_async_copy(mask, IM, lsem.at[2]),
        pltpu.make_async_copy(dirich, DM, lsem.at[3]),
        pltpu.make_async_copy(forcing, F.at[:, :, pl.ds(HALO, rows)], lsem.at[4]),
        pltpu.make_async_copy(observed, O.at[:, :, pl.ds(HALO, rows)], lsem.at[5]),
    ]
    for copy in loads:
        copy.start()

    barrier = pltpu.get_barrier_semaphore()
    for dx, dy in DIRS:
        @pl.when(has(dx, dy))
        def _():
            pl.semaphore_signal(barrier, inc=1, device_id=(gx + dx, gy + dy), device_id_type=MESH)

    lane = lax.broadcasted_iota(jnp.int32, (8, LANES), 1)
    low8 = (lane & 8) == 0
    left = lane < 64
    zero = jnp.zeros((8, LANES), jnp.float32)

    def roll(v, k):
        k = k % LANES
        return pltpu.roll(v, k, axis=1) if k else v

    for dx in (-1, 1):
        edge = pl.ds(0, 8) if dx < 0 else pl.ds(end, 8)

        @pl.when(lacks(dx, 0))
        def _():
            for t in range(EP):
                for c in range(2):
                    F[t, c, edge] = zero
                    O[t, c, edge] = zero
            for k in range(3):
                K[k, edge] = zero
        for dy in (-1, 1):
            @pl.when(lacks(dx, dy))
            def _():
                for k in range(3):
                    PS[0 if dy < 0 else 1, k, edge] = zero
    for dy in (-1, 1):
        @pl.when(lacks(0, dy))
        def _():
            PS[0 if dy < 0 else 1, :, pl.ds(HALO, rows)] = jnp.zeros((3, rows, LANES), jnp.float32)
    for m in range(2):
        for k in range(2):
            E[m, k, pl.ds(0, 8)] = zero
            E[m, k, pl.ds(ext + 8, 8)] = zero
    for b in range(2):
        for t in range(EP + 1):
            for c in range(2):
                for s in range(3):
                    D[b, t, c, s, pl.ds(0, 8)] = zero
                    D[b, t, c, s, pl.ds(ext + 8, 8)] = zero

    count = (1 + (gx > 0).astype(jnp.int32) + (gx < nx - 1).astype(jnp.int32)) * (
        1 + (gy > 0).astype(jnp.int32) + (gy < ny - 1).astype(jnp.int32)) - 1
    pl.semaphore_wait(barrier, count)

    def descs(d, stage):
        dx, dy = DIRS[d]
        target = (gx + dx, gy + dy)
        if dx == 0:
            src, dst = pl.ds(HALO, rows), pl.ds(HALO, rows)
        elif dx < 0:
            src, dst = pl.ds(HALO, 8), pl.ds(end, 8)
        else:
            src, dst = pl.ds(rows, 8), pl.ds(0, 8)
        if dy == 0:
            if stage == 0:
                pairs = [(0, F.at[:, :, src], F.at[:, :, dst]), (1, K.at[:, src], K.at[:, dst])]
            else:
                pairs = [(2, O.at[:, :, src], O.at[:, :, dst])]
        else:
            side = 0 if dy > 0 else 1
            part = pl.ds(0, 2) if stage == 0 else pl.ds(2, 1)
            pairs = [(0 if stage == 0 else 2, PK.at[part, src], PS.at[side, part, dst])]
        return [
            (j, pltpu.make_async_remote_copy(
                src_ref=s, dst_ref=q, send_sem=ssem.at[d, j], recv_sem=rsem.at[d, j],
                device_id=target, device_id_type=MESH))
            for j, s, q in pairs
        ]

    def send(d, stage, only=None):
        @pl.when(has(*DIRS[d]))
        def _():
            for j, copy in descs(d, stage):
                if only is None or j == only:
                    copy.start()

    def receive(d, stage):
        dx, dy = DIRS[d]

        @pl.when(has(-dx, -dy))
        def _():
            for _, copy in descs(d, stage):
                copy.wait_recv()

    def sent(d, stage):
        @pl.when(has(*DIRS[d]))
        def _():
            for _, copy in descs(d, stage):
                copy.wait_send()

    def at(r, off=0):
        return pl.ds(pl.multiple_of(r * 8, 8) + off, 8)

    def pack(get):
        out = None
        for t in range(EP):
            for c in range(2):
                g = c * EP + t
                v = roll(get(t, c), 16 * g + 8)
                out = v if out is None else jnp.where((lane >> 4) == g, v, out)
        return out

    def pack_coef(r):
        out = roll(K[0, at(r)], 8)
        out = jnp.where((lane >> 4) == 1, roll(K[1, at(r)], 24), out)
        return jnp.where((lane >> 4) == 2, roll(K[2, at(r)], 40), out)

    for copy in loads[:5]:
        copy.wait()
    for d in (0, 1):
        send(d, 0, 0)

    @pl.loop(0, own_tiles)
    def _(r):
        m = IM[at(r)]
        drag = jnp.where(m == 2, FM[at(r)], jnp.where(m == 0, FREE_DRAG, 0.0))
        K[1, at(r + 1)] = drag
        K[2, at(r + 1)] = (1 - DM[at(r)]).astype(jnp.float32)

    for d in (0, 1):
        send(d, 0, 1)

    @pl.loop(1, own_tiles + 1)
    def _(r):
        PK[0, at(r)] = pack(lambda t, c: F[t, c, at(r)])
        PK[1, at(r)] = pack_coef(r)

    for d in range(2, 8):
        send(d, 0)
    loads[5].wait()
    for d in (0, 1):
        send(d, 1)

    @pl.loop(1, own_tiles + 1)
    def _(r):
        PK[2, at(r)] = pack(lambda t, c: O[t, c, at(r)])

    for d in range(2, 8):
        send(d, 1)

    for d in range(8):
        receive(d, 0)

    def strips(k, r, own):
        sl = jnp.where(low8, PS[0, k, at(r)], own)
        sr = jnp.where(low8, own, PS[1, k, at(r)])
        return sl, sr

    def spread(sl, sr):
        return jnp.where(left, sl, roll(sr, 64)), jnp.where(left, roll(sl, 64), sr)

    @pl.loop(0, tiles)
    def _(r):
        E[0, 0, at(r, 8)] = K[0, at(r)]
        E[0, 1, at(r, 8)] = K[1, at(r)]
        sl, sr = strips(1, r, pack_coef(r))
        for k in range(3):
            v = jnp.where(lane < 16, roll(sl, -16 * k),
                          jnp.where((lane >> 4) == 4, roll(sr, 64 - 16 * k), 0.0))
            v = v + roll(v, 16)
            v = v + roll(v, 32)
            if k < 2:
                E[1, k, at(r, 8)] = v
            else:
                FRV[at(r)] = v

    first_scale, weights = chebyshev_weights()

    @pl.loop(0, tiles)
    def _(r):
        for m in range(2):
            e0 = E[m, 0, at(r, 8)]
            en = E[m, 0, at(r, 9)]
            es = E[m, 0, at(r, 7)]
            ee = roll(e0, -1)
            ew = roll(e0, 1)
            q = E[m, 1, at(r, 8)] + E[m, 1, at(r, 7)]
            drag = 0.25 * (q + roll(q, 1))
            free = K[2, at(r)] if m == 0 else FRV[at(r)]
            ap, am = 0.5 * (e0 + en), 0.5 * (e0 + es)
            bp, bm = 0.5 * (e0 + ee), 0.5 * (e0 + ew)
            asum, bsum = ap + am, bp + bm
            du = 4.0 * asum + bsum + drag
            dv = asum + 4.0 * bsum + drag
            n2, n4, s2, s4 = 0.5 * en, 0.25 * en, 0.5 * es, 0.25 * es
            e2, e4, w2, w4 = 0.5 * ee, 0.25 * ee, 0.5 * ew, 0.25 * ew
            vals = (
                du, 4.0 * ap, 4.0 * am, bp, bm, n2 + e4, n2 + w4, s2 + e4, s2 + w4,
                free / (du + 1.0 - free),
                dv, ap, am, 4.0 * bp, 4.0 * bm, n4 + e2, n4 + w2, s4 + e2, s4 + w2,
                free / (dv + 1.0 - free),
            )
            for k, v in enumerate(vals):
                KF[m, k, at(r)] = v

    def put(buf, t, c, r, d):
        D[buf, t, c, 0, at(r, 8)] = d
        D[buf, t, c, 1, at(r, 8)] = roll(d, -1)
        D[buf, t, c, 2, at(r, 8)] = roll(d, 1)

    def begin(t, r, iv, b):
        for c in range(2):
            d = iv[c] * b[c] * first_scale
            R[t, c, at(r)] = b[c]
            X[t, c, at(r)] = d
            put(0, t, c, r, d)

    def sweep(k, lo, hi):
        src, dst = k % 2, 1 - k % 2
        wa, wb = weights[k]
        last = k == SWEEPS - 1

        @pl.loop(lo, hi)
        def _(r):
            for t in range(EP + 1):
                m = 0 if t < EP else 1
                cf = lambda i: KF[m, i, at(r)]
                w = [[[D[src, t, c, s, at(r, 8 + o)] for o in (0, 1, -1)] for s in range(3)]
                     for c in range(2)]
                for c in range(2):
                    a, x = w[c], w[1 - c]
                    o = 10 * c
                    res = R[t, c, at(r)]
                    p1 = cf(o + 1) * a[0][1] + cf(o + 2) * a[0][2]
                    p2 = cf(o + 3) * a[1][0] + cf(o + 4) * a[2][0]
                    p3 = cf(o + 5) * x[1][1] - cf(o + 6) * x[2][1]
                    p4 = cf(o + 8) * x[2][2] - cf(o + 7) * x[1][2]
                    res = (res - cf(o) * a[0][0]) + ((p1 + p2) + (p3 + p4))
                    d = wa * a[0][0] + wb * (cf(o + 9) * res)
                    X[t, c, at(r)] = X[t, c, at(r)] + d
                    if not last:
                        R[t, c, at(r)] = res
                        put(dst, t, c, r, d)

    @pl.loop(0, tiles)
    def _(r):
        iv = [[KF[m, 9, at(r)], KF[m, 19, at(r)]] for m in range(2)]
        free = K[2, at(r)]
        for t in range(EP):
            begin(t, r, iv[0], [free * F[t, c, at(r)] for c in range(2)])
        u, v = spread(*strips(0, r, pack(lambda t, c: F[t, c, at(r)])))
        fr = FRV[at(r)]
        begin(EP, r, iv[1], [fr * u, fr * v])

    for k in range(SWEEPS):
        sweep(k, 0, tiles)

    for d in range(8):
        receive(d, 1)

    near, far = lane < 4, lane >= LANES - 4

    @pl.loop(0, tiles)
    def _(r):
        iv = [[KF[m, 9, at(r)], KF[m, 19, at(r)]] for m in range(2)]
        free = K[2, at(r)]
        side = [X[EP, c, at(r)] for c in range(2)]
        vel = [[None, None] for _ in range(EP)]
        for t in range(EP):
            for c in range(2):
                x = X[t, c, at(r)]
                x = jnp.where(near, roll(side[c], -16 * t - 8), x)
                x = jnp.where(far, roll(side[c], 56 - 16 * t), x)
                vel[t][c] = x
                VO[t, c, at(r)] = x
        p = pack(lambda t, c: vel[t][c])
        own = spread(p, p)
        mine = low8 != left
        obs = spread(*strips(2, r, pack(lambda t, c: O[t, c, at(r)])))
        fr = FRV[at(r)]
        sv = [jnp.where(mine, own[c], side[c]) for c in range(2)]
        for c in range(2):
            B2[c, at(r)] = sv[c]
        for t in range(EP):
            begin(t, r, iv[0], [free * (vel[t][c] - O[t, c, at(r)]) for c in range(2)])
        begin(EP, r, iv[1], [fr * (sv[c] - obs[c]) for c in range(2)])

    out_copy = pltpu.make_async_copy(VO.at[:, :, pl.ds(HALO, rows)], vel_out, osem.at[0])
    out_copy.start()

    for k in range(SWEEPS):
        sweep(k, 0 if k < SWEEPS - 1 else 1, tiles)

    @pl.loop(1, tiles)
    def _(r):
        p = None
        for t in range(EP):
            for c in range(2):
                q = X[t, c, at(r)] * VO[t, c, at(r)]
                p = q if p is None else p + q
        s = X[EP, 0, at(r)] * B2[0, at(r)] + X[EP, 1, at(r)] * B2[1, at(r)]
        s = s + roll(s, 16)
        s = s + roll(s, 32)
        p = jnp.where(near, roll(s, -56), p)
        p = jnp.where(far, roll(s, 8), p)
        nxt = jnp.where(lane == LANES - 1, roll(s, 7), roll(p, -1))
        PD[at(r)] = p + nxt

    @pl.loop(0, own_tiles)
    def _(r):
        q = PD[at(r, 8)] + PD[at(r, 9)]
        GO[at(r)] = jnp.where(IM[at(r)] == 2, -0.25 * q, 0.0)

    grad_copy = pltpu.make_async_copy(GO, grad_out, osem.at[1])
    grad_copy.start()
    for d in range(8):
        sent(d, 0)
        sent(d, 1)
    out_copy.wait()
    grad_copy.wait()


def body(forcing, observed, viscosity, friction, ice_mask, dirichlet):
    rows = viscosity.shape[0]
    ext = rows + 2 * HALO
    f32 = jnp.float32
    V = pltpu.VMEM
    grid = (rows, LANES)
    velocity, gradient = pl.pallas_call(
        lambda *refs: kernel(rows, *refs),
        out_shape=(
            jax.ShapeDtypeStruct(forcing.shape, f32),
            jax.ShapeDtypeStruct(grid, f32),
        ),
        in_specs=[pl.BlockSpec(memory_space=pl.ANY)] * 6,
        out_specs=(pl.BlockSpec(memory_space=pl.ANY),) * 2,
        scratch_shapes=[
            V((EP, 2, ext, LANES), f32),
            V((EP, 2, ext, LANES), f32),
            V((3, ext, LANES), f32),
            V(grid, f32), V(grid, jnp.int32), V(grid, jnp.int32),
            V((3, ext, LANES), f32),
            V((2, 3, ext, LANES), f32),
            V((2, 2, ext + 16, LANES), f32),
            V((ext, LANES), f32),
            V((2, NCOEF, ext, LANES), f32),
            V((2, EP + 1, 2, 3, ext + 16, LANES), f32),
            V((EP + 1, 2, ext, LANES), f32),
            V((EP + 1, 2, ext, LANES), f32),
            V((2, ext, LANES), f32),
            V((EP, 2, ext, LANES), f32),
            V((ext, LANES), f32),
            V((8, LANES), f32),
            V(grid, f32),
            pltpu.SemaphoreType.DMA((6,)),
            pltpu.SemaphoreType.DMA((2,)),
            pltpu.SemaphoreType.DMA((8, 3)),
            pltpu.SemaphoreType.DMA((8, 3)),
        ],
        compiler_params=pltpu.CompilerParams(
            collective_id=0, has_side_effects=True, vmem_limit_bytes=24 * 1024 * 1024
        ),
        cost_estimate=pl.CostEstimate(flops=40_000_000, bytes_accessed=1_000_000, transcendentals=0),
    )(forcing, observed, viscosity, friction, ice_mask, dirichlet)
    return velocity, gradient


def solution(mesh):
    wide, flat = P(None, None, "gx", "gy"), P("gx", "gy")
    return jax.shard_map(
        body,
        mesh=mesh,
        in_specs=(wide, wide, flat, flat, flat, flat),
        out_specs=(wide, flat),
        check_vma=False,
    )
```

```python
import jax
import jax.numpy as jnp
from jax import lax
from jax.experimental import pallas as pl
from jax.experimental.pallas import tpu as pltpu
from jax.sharding import PartitionSpec as P

SWEEPS = 3
UPPER_BOUND = 2.4
LOWER_BOUND = 0.05
FREE_DRAG = 4.0
HALO = 8
LANES = 128
EP = 4
NCOEF = 20
MESH = pl.DeviceIdType.MESH
DIRS = ((-1, 0), (1, 0), (0, -1), (0, 1), (-1, -1), (-1, 1), (1, -1), (1, 1))


def chebyshev_weights():
    centre = 0.5 * (UPPER_BOUND + LOWER_BOUND)
    half = 0.5 * (UPPER_BOUND - LOWER_BOUND)
    ratio = centre / half
    now = 1.0 / ratio
    pairs = []
    for _ in range(SWEEPS):
        following = 1.0 / (2.0 * ratio - now)
        pairs.append((following * now, 2.0 * following / half))
        now = following
    return 1.0 / centre, pairs


def kernel(rows, forcing, observed, visc, fric, mask, dirich, vel_out, grad_out,
           F, O, K, FM, IM, DM, PK, PS, E, FRV, KF, D0, D1, R, X, B2, VO, PD, PT, GO,
           lsem, osem, ssem, rsem):
    gx, gy = lax.axis_index("gx"), lax.axis_index("gy")
    nx, ny = lax.axis_size("gx"), lax.axis_size("gy")
    ext = rows + 2 * HALO
    tiles = ext // 8
    own_tiles = rows // 8
    end = rows + HALO

    def has(dx, dy):
        cond = None
        for idx, size, step in ((gx, nx, dx), (gy, ny, dy)):
            if step:
                here = idx > 0 if step < 0 else idx < size - 1
                cond = here if cond is None else jnp.logical_and(cond, here)
        return cond

    def lacks(dx, dy):
        return jnp.logical_not(has(dx, dy))

    loads = [
        pltpu.make_async_copy(visc, K.at[0, pl.ds(HALO, rows)], lsem.at[0]),
        pltpu.make_async_copy(fric, FM, lsem.at[1]),
        pltpu.make_async_copy(mask, IM, lsem.at[2]),
        pltpu.make_async_copy(dirich, DM, lsem.at[3]),
        pltpu.make_async_copy(forcing, F.at[:, :, pl.ds(HALO, rows)], lsem.at[4]),
        pltpu.make_async_copy(observed, O.at[:, :, pl.ds(HALO, rows)], lsem.at[5]),
    ]
    for copy in loads:
        copy.start()

    barrier = pltpu.get_barrier_semaphore()
    for dx, dy in DIRS:
        @pl.when(has(dx, dy))
        def _():
            pl.semaphore_signal(barrier, inc=1, device_id=(gx + dx, gy + dy), device_id_type=MESH)

    lane = lax.broadcasted_iota(jnp.int32, (8, LANES), 1)
    low8 = (lane & 8) == 0
    left = lane < 64
    zero = jnp.zeros((8, LANES), jnp.float32)

    def roll(v, k):
        k = k % LANES
        return pltpu.roll(v, k, axis=1) if k else v

    for dx in (-1, 1):
        edge = pl.ds(0, 8) if dx < 0 else pl.ds(end, 8)

        @pl.when(lacks(dx, 0))
        def _():
            for t in range(EP):
                for c in range(2):
                    F[t, c, edge] = zero
                    O[t, c, edge] = zero
            for k in range(3):
                K[k, edge] = zero
        for dy in (-1, 1):
            @pl.when(lacks(dx, dy))
            def _():
                for k in range(3):
                    PS[0 if dy < 0 else 1, k, edge] = zero
    for dy in (-1, 1):
        @pl.when(lacks(0, dy))
        def _():
            PS[0 if dy < 0 else 1, :, pl.ds(HALO, rows)] = jnp.zeros((3, rows, LANES), jnp.float32)
    for m in range(2):
        for k in range(2):
            E[m, k, pl.ds(0, 8)] = zero
            E[m, k, pl.ds(ext + 8, 8)] = zero
    for D in (D0, D1):
        for t in range(EP + 1):
            for c in range(2):
                for s in range(3):
                    D[t, c, s, pl.ds(0, 8)] = zero
                    D[t, c, s, pl.ds(ext + 8, 8)] = zero

    count = (1 + (gx > 0).astype(jnp.int32) + (gx < nx - 1).astype(jnp.int32)) * (
        1 + (gy > 0).astype(jnp.int32) + (gy < ny - 1).astype(jnp.int32)) - 1
    pl.semaphore_wait(barrier, count)

    def descs(d, stage, only=None):
        dx, dy = DIRS[d]
        target = (gx + dx, gy + dy)
        if dx == 0:
            src, dst = pl.ds(HALO, rows), pl.ds(HALO, rows)
        elif dx < 0:
            src, dst = pl.ds(HALO, 8), pl.ds(end, 8)
        else:
            src, dst = pl.ds(rows, 8), pl.ds(0, 8)
        if dy == 0:
            if stage == 0:
                pairs = [(0, F.at[:, :, src], F.at[:, :, dst]), (1, K.at[:, src], K.at[:, dst])]
            else:
                pairs = [(2, O.at[:, :, src], O.at[:, :, dst])]
        else:
            side = 0 if dy > 0 else 1
            part = pl.ds(0, 2) if stage == 0 else pl.ds(2, 1)
            pairs = [(0 if stage == 0 else 2, PK.at[part, src], PS.at[side, part, dst])]
        return [
            (j, pltpu.make_async_remote_copy(
                src_ref=s, dst_ref=q, send_sem=ssem.at[d, j], recv_sem=rsem.at[d, j],
                device_id=target, device_id_type=MESH))
            for j, s, q in pairs
            if only is None or j == only
        ]

    def send(d, stage, only=None):
        @pl.when(has(*DIRS[d]))
        def _():
            for _, copy in descs(d, stage, only):
                copy.start()

    def receive(d, stage):
        dx, dy = DIRS[d]

        @pl.when(has(-dx, -dy))
        def _():
            for _, copy in descs(d, stage):
                copy.wait_recv()

    def sent(d, stage):
        @pl.when(has(*DIRS[d]))
        def _():
            for _, copy in descs(d, stage):
                copy.wait_send()

    def at(r, off=0):
        if isinstance(r, int):
            return pl.ds(r * 8 + off, 8)
        return pl.ds(pl.multiple_of(r * 8, 8) + off, 8)

    def pack(get):
        out = None
        for t in range(EP):
            for c in range(2):
                g = c * EP + t
                v = roll(get(t, c), 16 * g + 8)
                out = v if out is None else jnp.where((lane >> 4) == g, v, out)
        return out

    def pack_coef(r):
        out = roll(K[0, at(r)], 8)
        out = jnp.where((lane >> 4) == 1, roll(K[1, at(r)], 24), out)
        return jnp.where((lane >> 4) == 2, roll(K[2, at(r)], 40), out)

    for copy in loads[:5]:
        copy.wait()
    for d in (0, 1):
        send(d, 0, 0)

    @pl.loop(0, own_tiles, unroll=True)
    def _(r):
        m = IM[at(r)]
        drag = jnp.where(m == 2, FM[at(r)], jnp.where(m == 0, FREE_DRAG, 0.0))
        K[1, at(r + 1)] = drag
        K[2, at(r + 1)] = (1 - DM[at(r)]).astype(jnp.float32)

    for d in (0, 1):
        send(d, 0, 1)

    @pl.loop(1, own_tiles + 1, unroll=True)
    def _(r):
        PK[0, at(r)] = pack(lambda t, c: F[t, c, at(r)])
        PK[1, at(r)] = pack_coef(r)

    for d in range(2, 8):
        send(d, 0)
    loads[5].wait()
    for d in (0, 1):
        send(d, 1)

    @pl.loop(1, own_tiles + 1, unroll=True)
    def _(r):
        PK[2, at(r)] = pack(lambda t, c: O[t, c, at(r)])

    for d in range(2, 8):
        send(d, 1)

    for d in range(8):
        receive(d, 0)

    def strips(k, r, own):
        sl = jnp.where(low8, PS[0, k, at(r)], own)
        sr = jnp.where(low8, own, PS[1, k, at(r)])
        return sl, sr

    def spread(sl, sr):
        return jnp.where(left, sl, roll(sr, 64)), jnp.where(left, roll(sl, 64), sr)

    @pl.loop(0, tiles, unroll=True)
    def _(r):
        E[0, 0, at(r, 8)] = K[0, at(r)]
        E[0, 1, at(r, 8)] = K[1, at(r)]
        sl, sr = strips(1, r, pack_coef(r))
        for k in range(3):
            v = jnp.where(lane < 16, roll(sl, -16 * k),
                          jnp.where((lane >> 4) == 4, roll(sr, 64 - 16 * k), 0.0))
            v = v + roll(v, 16)
            v = v + roll(v, 32)
            if k < 2:
                E[1, k, at(r, 8)] = v
            else:
                FRV[at(r)] = v

    first_scale, weights = chebyshev_weights()

    @pl.loop(0, tiles, unroll=True)
    def _(r):
        for m in range(2):
            e0 = E[m, 0, at(r, 8)]
            en = E[m, 0, at(r, 9)]
            es = E[m, 0, at(r, 7)]
            ee = roll(e0, -1)
            ew = roll(e0, 1)
            q = E[m, 1, at(r, 8)] + E[m, 1, at(r, 7)]
            drag = 0.25 * (q + roll(q, 1))
            free = K[2, at(r)] if m == 0 else FRV[at(r)]
            ap, am = 0.5 * (e0 + en), 0.5 * (e0 + es)
            bp, bm = 0.5 * (e0 + ee), 0.5 * (e0 + ew)
            asum, bsum = ap + am, bp + bm
            du = 4.0 * asum + bsum + drag
            dv = asum + 4.0 * bsum + drag
            n2, n4, s2, s4 = 0.5 * en, 0.25 * en, 0.5 * es, 0.25 * es
            e2, e4, w2, w4 = 0.5 * ee, 0.25 * ee, 0.5 * ew, 0.25 * ew
            vals = (
                du, 4.0 * ap, 4.0 * am, bp, bm, n2 + e4, n2 + w4, s2 + e4, s2 + w4,
                free / (du + 1.0 - free),
                dv, ap, am, 4.0 * bp, 4.0 * bm, n4 + e2, n4 + w2, s4 + e2, s4 + w2,
                free / (dv + 1.0 - free),
            )
            for k, v in enumerate(vals):
                KF[m, k, at(r)] = v

    def put(buf, t, c, r, d):
        buf[t, c, 0, at(r, 8)] = d
        buf[t, c, 1, at(r, 8)] = roll(d, -1)
        buf[t, c, 2, at(r, 8)] = roll(d, 1)

    def begin(t, r, iv, b):
        for c in range(2):
            d = iv[c] * b[c] * first_scale
            R[t, c, at(r)] = b[c]
            X[t, c, at(r)] = d
            put(D0, t, c, r, d)

    def sweep(k, lo, hi):
        src, dst = (D0, D1) if k % 2 == 0 else (D1, D0)
        wa, wb = weights[k]
        last = k == SWEEPS - 1

        @pl.loop(lo, hi, unroll=True)
        def _(r):
            for t in range(EP + 1):
                if t == 0 or t == EP:
                    coef = [KF[0 if t < EP else 1, i, at(r)] for i in range(NCOEF)]
                cf = lambda i: coef[i]
                w = [[[src[t, c, s, at(r, 8 + o)] for o in (0, 1, -1)] for s in range(3)]
                     for c in range(2)]
                for c in range(2):
                    a, x = w[c], w[1 - c]
                    o = 10 * c
                    res = R[t, c, at(r)]
                    p1 = cf(o + 1) * a[0][1] + cf(o + 2) * a[0][2]
                    p2 = cf(o + 3) * a[1][0] + cf(o + 4) * a[2][0]
                    p3 = cf(o + 5) * x[1][1] - cf(o + 6) * x[2][1]
                    p4 = cf(o + 8) * x[2][2] - cf(o + 7) * x[1][2]
                    res = (res - cf(o) * a[0][0]) + ((p1 + p2) + (p3 + p4))
                    d = wa * a[0][0] + wb * (cf(o + 9) * res)
                    X[t, c, at(r)] = X[t, c, at(r)] + d
                    if not last:
                        R[t, c, at(r)] = res
                        put(dst, t, c, r, d)

    @pl.loop(0, tiles, unroll=True)
    def _(r):
        iv = [[KF[m, 9, at(r)], KF[m, 19, at(r)]] for m in range(2)]
        free = K[2, at(r)]
        for t in range(EP):
            begin(t, r, iv[0], [free * F[t, c, at(r)] for c in range(2)])
        u, v = spread(*strips(0, r, pack(lambda t, c: F[t, c, at(r)])))
        fr = FRV[at(r)]
        begin(EP, r, iv[1], [fr * u, fr * v])

    for k in range(SWEEPS):
        sweep(k, 0, tiles)

    for d in range(8):
        receive(d, 1)

    near, far = lane < 4, lane >= LANES - 4

    @pl.loop(0, tiles, unroll=True)
    def _(r):
        iv = [[KF[m, 9, at(r)], KF[m, 19, at(r)]] for m in range(2)]
        free = K[2, at(r)]
        side = [X[EP, c, at(r)] for c in range(2)]
        vel = [[None, None] for _ in range(EP)]
        for t in range(EP):
            for c in range(2):
                x = X[t, c, at(r)]
                x = jnp.where(near, roll(side[c], -16 * t - 8), x)
                x = jnp.where(far, roll(side[c], 56 - 16 * t), x)
                vel[t][c] = x
                VO[t, c, at(r)] = x
        p = pack(lambda t, c: vel[t][c])
        own = spread(p, p)
        mine = low8 != left
        obs = spread(*strips(2, r, pack(lambda t, c: O[t, c, at(r)])))
        fr = FRV[at(r)]
        sv = [jnp.where(mine, own[c], side[c]) for c in range(2)]
        for c in range(2):
            B2[c, at(r)] = sv[c]
        for t in range(EP):
            begin(t, r, iv[0], [free * (vel[t][c] - O[t, c, at(r)]) for c in range(2)])
        begin(EP, r, iv[1], [fr * (sv[c] - obs[c]) for c in range(2)])

    out_copy = pltpu.make_async_copy(VO.at[:, :, pl.ds(HALO, rows)], vel_out, osem.at[0])
    out_copy.start()

    for k in range(SWEEPS):
        sweep(k, 0 if k < SWEEPS - 1 else 1, tiles)

    @pl.loop(1, tiles, unroll=True)
    def _(r):
        p = None
        for t in range(EP):
            for c in range(2):
                q = X[t, c, at(r)] * VO[t, c, at(r)]
                p = q if p is None else p + q
        s = X[EP, 0, at(r)] * B2[0, at(r)] + X[EP, 1, at(r)] * B2[1, at(r)]
        s = s + roll(s, 16)
        s = s + roll(s, 32)
        p = jnp.where(near, roll(s, -56), p)
        p = jnp.where(far, roll(s, 8), p)
        nxt = jnp.where(lane == LANES - 1, roll(s, 7), roll(p, -1))
        PD[at(r)] = p + nxt

    @pl.loop(0, own_tiles, unroll=True)
    def _(r):
        q = PD[at(r, 8)] + PD[at(r, 9)]
        GO[at(r)] = jnp.where(IM[at(r)] == 2, -0.25 * q, 0.0)

    grad_copy = pltpu.make_async_copy(GO, grad_out, osem.at[1])
    grad_copy.start()
    for d in range(8):
        sent(d, 0)
        sent(d, 1)
    out_copy.wait()
    grad_copy.wait()


def body(forcing, observed, viscosity, friction, ice_mask, dirichlet):
    rows = viscosity.shape[0]
    ext = rows + 2 * HALO
    f32 = jnp.float32
    V = pltpu.VMEM
    grid = (rows, LANES)
    velocity, gradient = pl.pallas_call(
        lambda *refs: kernel(rows, *refs),
        out_shape=(
            jax.ShapeDtypeStruct(forcing.shape, f32),
            jax.ShapeDtypeStruct(grid, f32),
        ),
        in_specs=[pl.BlockSpec(memory_space=pltpu.HBM)] * 6,
        out_specs=(pl.BlockSpec(memory_space=pltpu.HBM),) * 2,
        scratch_shapes=[
            V((EP, 2, ext, LANES), f32),
            V((EP, 2, ext, LANES), f32),
            V((3, ext, LANES), f32),
            V(grid, f32), V(grid, jnp.int32), V(grid, jnp.int32),
            V((3, ext, LANES), f32),
            V((2, 3, ext, LANES), f32),
            V((2, 2, ext + 16, LANES), f32),
            V((ext, LANES), f32),
            V((2, NCOEF, ext, LANES), f32),
            V((EP + 1, 2, 3, ext + 16, LANES), f32),
            V((EP + 1, 2, 3, ext + 16, LANES), f32),
            V((EP + 1, 2, ext, LANES), f32),
            V((EP + 1, 2, ext, LANES), f32),
            V((2, ext, LANES), f32),
            V((EP, 2, ext, LANES), f32),
            V((ext, LANES), f32),
            V((8, LANES), f32),
            V(grid, f32),
            pltpu.SemaphoreType.DMA((6,)),
            pltpu.SemaphoreType.DMA((2,)),
            pltpu.SemaphoreType.DMA((8, 3)),
            pltpu.SemaphoreType.DMA((8, 3)),
        ],
        compiler_params=pltpu.CompilerParams(
            collective_id=0, has_side_effects=True, vmem_limit_bytes=63 * 1024 * 1024
        ),
        cost_estimate=pl.CostEstimate(flops=40_000_000, bytes_accessed=1_000_000, transcendentals=0),
    )(forcing, observed, viscosity, friction, ice_mask, dirichlet)
    return velocity, gradient


def solution(mesh):
    wide, flat = P(None, None, "gx", "gy"), P("gx", "gy")
    return jax.shard_map(
        body,
        mesh=mesh,
        in_specs=(wide, wide, flat, flat, flat, flat),
        out_specs=(wide, flat),
        check_vma=False,
    )
```

```python
import jax
import jax.numpy as jnp
from jax import lax
from jax.experimental import pallas as pl
from jax.experimental.pallas import tpu as pltpu
from jax.sharding import PartitionSpec as P

SWEEPS = 3
UPPER_BOUND = 2.4
LOWER_BOUND = 0.05
FREE_DRAG = 4.0
HALO = 8
LANES = 128
EP = 4
NCOEF = 20
MESH = pl.DeviceIdType.MESH
DIRS = ((-1, 0), (1, 0), (0, -1), (0, 1), (-1, -1), (-1, 1), (1, -1), (1, 1))


def chebyshev_weights():
    centre = 0.5 * (UPPER_BOUND + LOWER_BOUND)
    half = 0.5 * (UPPER_BOUND - LOWER_BOUND)
    ratio = centre / half
    now = 1.0 / ratio
    pairs = []
    for _ in range(SWEEPS):
        following = 1.0 / (2.0 * ratio - now)
        pairs.append((following * now, 2.0 * following / half))
        now = following
    return 1.0 / centre, pairs


def kernel(rows, forcing, observed, visc, fric, mask, dirich, vel_out, grad_out,
           F, O, K, FM, IM, DM, PK, PS, E, FRV, KF, D0, D1, R, X, B2, VO, PD, PT,
           lsem, ssem, rsem):
    gx, gy = lax.axis_index("gx"), lax.axis_index("gy")
    nx, ny = lax.axis_size("gx"), lax.axis_size("gy")
    ext = rows + 2 * HALO
    tiles = ext // 8
    own_tiles = rows // 8
    end = rows + HALO

    def has(dx, dy):
        cond = None
        for idx, size, step in ((gx, nx, dx), (gy, ny, dy)):
            if step:
                here = idx > 0 if step < 0 else idx < size - 1
                cond = here if cond is None else jnp.logical_and(cond, here)
        return cond

    def lacks(dx, dy):
        return jnp.logical_not(has(dx, dy))

    loads = [
        pltpu.make_async_copy(visc, K.at[0, pl.ds(HALO, rows)], lsem.at[0]),
        pltpu.make_async_copy(fric, FM, lsem.at[1]),
        pltpu.make_async_copy(mask, IM, lsem.at[2]),
        pltpu.make_async_copy(dirich, DM, lsem.at[3]),
        pltpu.make_async_copy(forcing, F.at[:, :, pl.ds(HALO, rows)], lsem.at[4]),
        pltpu.make_async_copy(observed, O.at[:, :, pl.ds(HALO, rows)], lsem.at[5]),
    ]
    for copy in loads:
        copy.start()

    barrier = pltpu.get_barrier_semaphore()
    for dx, dy in DIRS:
        @pl.when(has(dx, dy))
        def _():
            pl.semaphore_signal(barrier, inc=1, device_id=(gx + dx, gy + dy), device_id_type=MESH)

    lane = lax.broadcasted_iota(jnp.int32, (8, LANES), 1)
    low8 = (lane & 8) == 0
    left = lane < 64
    zero = jnp.zeros((8, LANES), jnp.float32)

    def roll(v, k):
        k = k % LANES
        return pltpu.roll(v, k, axis=1) if k else v

    for dx in (-1, 1):
        edge = pl.ds(0, 8) if dx < 0 else pl.ds(end, 8)

        @pl.when(lacks(dx, 0))
        def _():
            for t in range(EP):
                for c in range(2):
                    F[t, c, edge] = zero
                    O[t, c, edge] = zero
            for k in range(3):
                K[k, edge] = zero
        for dy in (-1, 1):
            @pl.when(lacks(dx, dy))
            def _():
                for k in range(3):
                    PS[0 if dy < 0 else 1, k, edge] = zero
    for dy in (-1, 1):
        @pl.when(lacks(0, dy))
        def _():
            PS[0 if dy < 0 else 1, :, pl.ds(HALO, rows)] = jnp.zeros((3, rows, LANES), jnp.float32)
    for m in range(2):
        for k in range(2):
            E[m, k, pl.ds(0, 8)] = zero
            E[m, k, pl.ds(ext + 8, 8)] = zero
    for D in (D0, D1):
        for t in range(EP + 1):
            for c in range(2):
                for s in range(3):
                    D[t, c, s, pl.ds(0, 8)] = zero
                    D[t, c, s, pl.ds(ext + 8, 8)] = zero

    count = (1 + (gx > 0).astype(jnp.int32) + (gx < nx - 1).astype(jnp.int32)) * (
        1 + (gy > 0).astype(jnp.int32) + (gy < ny - 1).astype(jnp.int32)) - 1
    pl.semaphore_wait(barrier, count)

    def descs(d, stage, only=None):
        dx, dy = DIRS[d]
        target = (gx + dx, gy + dy)
        if dx == 0:
            src, dst = pl.ds(HALO, rows), pl.ds(HALO, rows)
        elif dx < 0:
            src, dst = pl.ds(HALO, 8), pl.ds(end, 8)
        else:
            src, dst = pl.ds(rows, 8), pl.ds(0, 8)
        if dy == 0:
            if stage == 0:
                pairs = [(0, F.at[:, :, src], F.at[:, :, dst]), (1, K.at[:, src], K.at[:, dst])]
            else:
                pairs = [(2, O.at[:, :, src], O.at[:, :, dst])]
        else:
            side = 0 if dy > 0 else 1
            part = pl.ds(0, 2) if stage == 0 else pl.ds(2, 1)
            pairs = [(0 if stage == 0 else 2, PK.at[part, src], PS.at[side, part, dst])]
        return [
            (j, pltpu.make_async_remote_copy(
                src_ref=s, dst_ref=q, send_sem=ssem.at[d, j], recv_sem=rsem.at[d, j],
                device_id=target, device_id_type=MESH))
            for j, s, q in pairs
            if only is None or j == only
        ]

    def send(d, stage, only=None):
        @pl.when(has(*DIRS[d]))
        def _():
            for _, copy in descs(d, stage, only):
                copy.start()

    def receive(d, stage):
        dx, dy = DIRS[d]

        @pl.when(has(-dx, -dy))
        def _():
            for _, copy in descs(d, stage):
                copy.wait_recv()

    def sent(d, stage):
        @pl.when(has(*DIRS[d]))
        def _():
            for _, copy in descs(d, stage):
                copy.wait_send()

    def at(r, off=0):
        if isinstance(r, int):
            return pl.ds(r * 8 + off, 8)
        return pl.ds(pl.multiple_of(r * 8, 8) + off, 8)

    def pack(get):
        out = None
        for t in range(EP):
            for c in range(2):
                g = c * EP + t
                v = roll(get(t, c), 16 * g + 8)
                out = v if out is None else jnp.where((lane >> 4) == g, v, out)
        return out

    def pack_coef(r):
        out = roll(K[0, at(r)], 8)
        out = jnp.where((lane >> 4) == 1, roll(K[1, at(r)], 24), out)
        return jnp.where((lane >> 4) == 2, roll(K[2, at(r)], 40), out)

    loads[4].wait()
    for d in (0, 1):
        send(d, 0, 0)
    for copy in loads[:4]:
        copy.wait()

    @pl.loop(0, own_tiles, unroll=True)
    def _(r):
        m = IM[at(r)]
        drag = jnp.where(m == 2, FM[at(r)], jnp.where(m == 0, FREE_DRAG, 0.0))
        K[1, at(r + 1)] = drag
        K[2, at(r + 1)] = (1 - DM[at(r)]).astype(jnp.float32)

    for d in (0, 1):
        send(d, 0, 1)

    @pl.loop(1, own_tiles + 1, unroll=True)
    def _(r):
        PK[0, at(r)] = pack(lambda t, c: F[t, c, at(r)])
        PK[1, at(r)] = pack_coef(r)

    for d in range(2, 8):
        send(d, 0)
    loads[5].wait()
    for d in (0, 1):
        send(d, 1)

    @pl.loop(1, own_tiles + 1, unroll=True)
    def _(r):
        PK[2, at(r)] = pack(lambda t, c: O[t, c, at(r)])

    for d in range(2, 8):
        send(d, 1)

    def strips(k, r, own):
        sl = jnp.where(low8, PS[0, k, at(r)], own)
        sr = jnp.where(low8, own, PS[1, k, at(r)])
        return sl, sr

    def spread(sl, sr):
        return jnp.where(left, sl, roll(sr, 64)), jnp.where(left, roll(sl, 64), sr)

    first_scale, weights = chebyshev_weights()

    def put(buf, t, c, r, d):
        buf[t, c, 0, at(r, 8)] = d
        buf[t, c, 1, at(r, 8)] = roll(d, -1)
        buf[t, c, 2, at(r, 8)] = roll(d, 1)

    def begin(t, r, iv, b):
        for c in range(2):
            d = iv[c] * b[c] * first_scale
            R[t, c, at(r)] = b[c]
            X[t, c, at(r)] = d
            put(D0, t, c, r, d)

    def coefs(m, r):
        e0 = E[m, 0, at(r, 8)]
        en = E[m, 0, at(r, 9)]
        es = E[m, 0, at(r, 7)]
        ee = roll(e0, -1)
        ew = roll(e0, 1)
        q = E[m, 1, at(r, 8)] + E[m, 1, at(r, 7)]
        drag = 0.25 * (q + roll(q, 1))
        free = K[2, at(r)] if m == 0 else FRV[at(r)]
        ap, am = 0.5 * (e0 + en), 0.5 * (e0 + es)
        bp, bm = 0.5 * (e0 + ee), 0.5 * (e0 + ew)
        asum, bsum = ap + am, bp + bm
        du = 4.0 * asum + bsum + drag
        dv = asum + 4.0 * bsum + drag
        n2, n4, s2, s4 = 0.5 * en, 0.25 * en, 0.5 * es, 0.25 * es
        e2, e4, w2, w4 = 0.5 * ee, 0.25 * ee, 0.5 * ew, 0.25 * ew
        vals = (
            du, 4.0 * ap, 4.0 * am, bp, bm, n2 + e4, n2 + w4, s2 + e4, s2 + w4,
            free / (du + 1.0 - free),
            dv, ap, am, 4.0 * bp, 4.0 * bm, n4 + e2, n4 + w2, s4 + e2, s4 + w2,
            free / (dv + 1.0 - free),
        )
        for k, v in enumerate(vals):
            KF[m, k, at(r)] = v

    def start_main(r):
        coefs(0, r)
        iv = [KF[0, 9, at(r)], KF[0, 19, at(r)]]
        free = K[2, at(r)]
        for t in range(EP):
            begin(t, r, iv, [free * F[t, c, at(r)] for c in range(2)])

    def fill_main(r):
        E[0, 0, at(r, 8)] = K[0, at(r)]
        E[0, 1, at(r, 8)] = K[1, at(r)]

    @pl.loop(1, own_tiles + 1, unroll=True)
    def _(r):
        fill_main(r)

    @pl.loop(2, own_tiles, unroll=True)
    def _(r):
        start_main(r)

    for d in range(8):
        receive(d, 0)

    for r in (0, tiles - 1):
        fill_main(r)
    for r in (0, 1, tiles - 2, tiles - 1):
        start_main(r)

    @pl.loop(0, tiles, unroll=True)
    def _(r):
        sl, sr = strips(1, r, pack_coef(r))
        for k in range(3):
            v = jnp.where(lane < 16, roll(sl, -16 * k),
                          jnp.where((lane >> 4) == 4, roll(sr, 64 - 16 * k), 0.0))
            v = v + roll(v, 16)
            v = v + roll(v, 32)
            if k < 2:
                E[1, k, at(r, 8)] = v
            else:
                FRV[at(r)] = v

    @pl.loop(0, tiles, unroll=True)
    def _(r):
        coefs(1, r)

    def sweep(k, lo, hi):
        src, dst = (D0, D1) if k % 2 == 0 else (D1, D0)
        wa, wb = weights[k]
        last = k == SWEEPS - 1

        @pl.loop(lo, hi, unroll=True)
        def _(r):
            for t in range(EP + 1):
                if t == 0 or t == EP:
                    coef = [KF[0 if t < EP else 1, i, at(r)] for i in range(NCOEF)]
                cf = lambda i: coef[i]
                w = [[[src[t, c, s, at(r, 8 + o)] for o in (0, 1, -1)] for s in range(3)]
                     for c in range(2)]
                for c in range(2):
                    a, x = w[c], w[1 - c]
                    o = 10 * c
                    res = R[t, c, at(r)]
                    p1 = cf(o + 1) * a[0][1] + cf(o + 2) * a[0][2]
                    p2 = cf(o + 3) * a[1][0] + cf(o + 4) * a[2][0]
                    p3 = cf(o + 5) * x[1][1] - cf(o + 6) * x[2][1]
                    p4 = cf(o + 8) * x[2][2] - cf(o + 7) * x[1][2]
                    res = (res - cf(o) * a[0][0]) + ((p1 + p2) + (p3 + p4))
                    d = wa * a[0][0] + wb * (cf(o + 9) * res)
                    X[t, c, at(r)] = X[t, c, at(r)] + d
                    if not last:
                        R[t, c, at(r)] = res
                        put(dst, t, c, r, d)

    @pl.loop(0, tiles, unroll=True)
    def _(r):
        iv = [KF[1, 9, at(r)], KF[1, 19, at(r)]]
        u, v = spread(*strips(0, r, pack(lambda t, c: F[t, c, at(r)])))
        fr = FRV[at(r)]
        begin(EP, r, iv, [fr * u, fr * v])

    for k in range(SWEEPS):
        sweep(k, 0, tiles)

    for d in range(8):
        receive(d, 1)

    near, far = lane < 4, lane >= LANES - 4

    @pl.loop(0, tiles, unroll=True)
    def _(r):
        iv = [[KF[m, 9, at(r)], KF[m, 19, at(r)]] for m in range(2)]
        free = K[2, at(r)]
        side = [X[EP, c, at(r)] for c in range(2)]
        vel = [[None, None] for _ in range(EP)]
        for t in range(EP):
            for c in range(2):
                x = X[t, c, at(r)]
                x = jnp.where(near, roll(side[c], -16 * t - 8), x)
                x = jnp.where(far, roll(side[c], 56 - 16 * t), x)
                vel[t][c] = x
                VO[t, c, at(r)] = x
        p = pack(lambda t, c: vel[t][c])
        own = spread(p, p)
        mine = low8 != left
        obs = spread(*strips(2, r, pack(lambda t, c: O[t, c, at(r)])))
        fr = FRV[at(r)]
        sv = [jnp.where(mine, own[c], side[c]) for c in range(2)]
        for c in range(2):
            B2[c, at(r)] = sv[c]
        for t in range(EP):
            begin(t, r, iv[0], [free * (vel[t][c] - O[t, c, at(r)]) for c in range(2)])
        begin(EP, r, iv[1], [fr * (sv[c] - obs[c]) for c in range(2)])

    @pl.loop(0, own_tiles, unroll=True)
    def _(r):
        for t in range(EP):
            for c in range(2):
                vel_out[t, c, at(r)] = VO[t, c, at(r, 8)]

    for k in range(SWEEPS):
        sweep(k, 0 if k < SWEEPS - 1 else 1, tiles)

    @pl.loop(1, tiles, unroll=True)
    def _(r):
        p = None
        for t in range(EP):
            for c in range(2):
                q = X[t, c, at(r)] * VO[t, c, at(r)]
                p = q if p is None else p + q
        s = X[EP, 0, at(r)] * B2[0, at(r)] + X[EP, 1, at(r)] * B2[1, at(r)]
        s = s + roll(s, 16)
        s = s + roll(s, 32)
        p = jnp.where(near, roll(s, -56), p)
        p = jnp.where(far, roll(s, 8), p)
        nxt = jnp.where(lane == LANES - 1, roll(s, 7), roll(p, -1))
        PD[at(r)] = p + nxt

    @pl.loop(0, own_tiles, unroll=True)
    def _(r):
        q = PD[at(r, 8)] + PD[at(r, 9)]
        grad_out[at(r)] = jnp.where(IM[at(r)] == 2, -0.25 * q, 0.0)

    for d in range(8):
        sent(d, 0)
        sent(d, 1)


def body(forcing, observed, viscosity, friction, ice_mask, dirichlet):
    rows = viscosity.shape[0]
    ext = rows + 2 * HALO
    f32 = jnp.float32
    V = pltpu.VMEM
    grid = (rows, LANES)
    velocity, gradient = pl.pallas_call(
        lambda *refs: kernel(rows, *refs),
        out_shape=(
            pltpu.VMEM(forcing.shape, f32),
            pltpu.VMEM(grid, f32),
        ),
        in_specs=[pl.BlockSpec(memory_space=pltpu.HBM)] * 6,
        out_specs=(pl.BlockSpec(memory_space=pltpu.VMEM),) * 2,
        scratch_shapes=[
            V((EP, 2, ext, LANES), f32),
            V((EP, 2, ext, LANES), f32),
            V((3, ext, LANES), f32),
            V(grid, f32), V(grid, jnp.int32), V(grid, jnp.int32),
            V((3, ext, LANES), f32),
            V((2, 3, ext, LANES), f32),
            V((2, 2, ext + 16, LANES), f32),
            V((ext, LANES), f32),
            V((2, NCOEF, ext, LANES), f32),
            V((EP + 1, 2, 3, ext + 16, LANES), f32),
            V((EP + 1, 2, 3, ext + 16, LANES), f32),
            V((EP + 1, 2, ext, LANES), f32),
            V((EP + 1, 2, ext, LANES), f32),
            V((2, ext, LANES), f32),
            V((EP, 2, ext, LANES), f32),
            V((ext, LANES), f32),
            V((8, LANES), f32),
            pltpu.SemaphoreType.DMA((6,)),
            pltpu.SemaphoreType.DMA((8, 3)),
            pltpu.SemaphoreType.DMA((8, 3)),
        ],
        compiler_params=pltpu.CompilerParams(
            collective_id=0, has_side_effects=True, vmem_limit_bytes=24576 * 1024
        ),
        cost_estimate=pl.CostEstimate(flops=40_000_000, bytes_accessed=1_000_000, transcendentals=0),
    )(*(pltpu.with_memory_space_constraint(a, pltpu.HBM) for a in (forcing, observed, viscosity, friction, ice_mask, dirichlet)))
    return velocity, gradient


def solution(mesh):
    wide, flat = P(None, None, "gx", "gy"), P("gx", "gy")
    return jax.shard_map(
        body,
        mesh=mesh,
        in_specs=(wide, wide, flat, flat, flat, flat),
        out_specs=(wide, flat),
        check_vma=False,
    )
```
